512 devices in a mesh: section: 32 (over y, x_lo, core), tp: 16 (over x_hi, z).
Axes of the slice: x: 4 (x_hi: 2, x_lo: 2; x = x_hi * 2 + x_lo), y: 8, z: 8, core: 2. Of those that a mesh axis runs over, the one named last changes fastest.
Arguments:
- acts: bfloat16 [32, 768, 12288], P('section', None, 'tp'), may hold values from -6 to 6
- plan: int32 [2, 32], replicated, may hold values from 0 to 1
- norm_gain: float32 [32, 2, 12288], P('section', None, 'tp'), may hold values from 0.25 to 1.75
- query_gain: float32 [32, 2, 12288], P('section', None, 'tp'), may hold values from 0.25 to 6
- key_gain: float32 [32, 2, 12288], P('section', None, 'tp'), may hold values from 0.25 to 6
- value_gain: float32 [32, 2, 12288], P('section', None, 'tp'), may hold values from 1 to 8
Outputs:
- final_acts: bfloat16 [32, 768, 12288], P('section', None, 'tp')
- stashed: bfloat16 [32, 2, 768, 12288], P('section', None, None, 'tp')
The draws below stay inside these ranges and needn't reach their ends.
All inputs are finite; a program needn't handle non-finite values.
Results may differ from the reference program's by a relative error of at most 0.012.
The reference program's roundings to bfloat16 on the way count: a program that leaves them out, or rounds other values in their place, can miss the bound.
Values may be sent and summed in bfloat16 or wider, within the bound.
No kernel may reach another device: no remote copies, remote signals or barrier semaphores. Data moves between devices by JAX's collectives and lax.ppermute only.
A program may use at most 64 MiB of HBM per device.

```python
import math
import jax
import jax.numpy as jnp
from jax import lax

D = 12288
HEAD = 128
HEADS = 96
SEQ = 768
STEPS = 2
LAPS = 2
SECTIONS = 32


def base_gains(key):
    return jnp.exp(jax.random.uniform(key, (SECTIONS, LAPS, D), jnp.float32, math.log(0.25), 0.0))


def draw_query_gain(key, part):
    key = jax.random.fold_in(key, 3)
    base = base_gains(key)
    return base


def draw_key_gain(key, part):
    key = jax.random.fold_in(key, 5)
    base = base_gains(key)
    return base


def place_ends(drawn, key, smallest, top_value):
    longest = drawn.shape.index(max(drawn.shape))
    spots = []
    for shift in (0, 1):
        where = [jax.random.randint(jax.random.fold_in(key, axis), (), 0, length) for axis, length in enumerate(drawn.shape)]
        where[longest] = (where[longest] + shift) % drawn.shape[longest]
        spots.append(tuple(where))
    return drawn.at[spots[0]].set(smallest).at[spots[1]].set(top_value)


def levels(rng, extent, split, low, high):
    factor_of = 1.0
    for axis_at, shards_of in split:
        steps = jax.random.uniform(jax.random.fold_in(jax.random.fold_in(rng, 6), axis_at), (shards_of,), jnp.float32, low / len(split), high / len(split))
        factor_of = factor_of * jnp.repeat(jnp.exp(steps), extent[axis_at] // shards_of).reshape((-1,) + (1,) * (len(extent) - 1 - axis_at))
    return factor_of


def noise(key, shape, spread, most, split=(), kind=jnp.bfloat16):
    gain = levels(key, shape, split, -0.22, 0.18) if split else 1.0
    result = jax.random.normal(key, shape, jnp.float32) * spread * gain
    return jnp.minimum(jnp.maximum(result, -most), most).astype(kind)


def setup_inputs(seed: int = 0) -> dict:
    seeds = jax.random.split(jax.random.key(seed), 7)
    acts = noise(seeds[0], (SECTIONS, SEQ, D), 1.0, 6.0, ((0, 32), (2, 16)))
    plan = place_ends(jax.random.randint(seeds[1], (STEPS, SECTIONS), 0, LAPS), jax.random.fold_in(seeds[1], 1), 0, LAPS - 1).astype(jnp.int32)
    norm_gain = jnp.clip(1.0 + 0.15 * jax.random.normal(seeds[2], (SECTIONS, LAPS, D), jnp.float32), 0.25, 1.75)
    query_gain = draw_query_gain(jax.random.fold_in(seeds[6], 71), 0)
    key_gain = draw_key_gain(jax.random.fold_in(seeds[6], 71), 0)
    value_gain = jnp.clip(jnp.exp(math.log(8.0) - 2.0794415 * jax.random.uniform(seeds[5], (SECTIONS, LAPS, D), jnp.float32) ** levels(seeds[5], (SECTIONS, LAPS, D), ((0, 32), (2, 16)), -0.2, 0.2)), 1.0, 8.0)
    return dict(acts=acts, plan=plan, norm_gain=norm_gain, query_gain=query_gain, key_gain=key_gain, value_gain=value_gain)


def mixer(x, norm_g, query_g, key_g, value_g):
    xf = x.astype(jnp.float32)
    mean_sq = lax.optimization_barrier(jnp.mean(xf * xf, axis=-1, keepdims=True))
    normed = xf * lax.rsqrt(mean_sq + 1e-05) * norm_g
    query = (normed * query_g).astype(jnp.bfloat16).reshape(SEQ, HEADS, HEAD)
    keys = (normed * key_g).astype(jnp.bfloat16).reshape(SEQ, HEADS, HEAD)
    values = normed.astype(jnp.bfloat16).reshape(SEQ, HEADS, HEAD)
    scores = jnp.einsum('qhd,khd->hqk', query.astype(jnp.float32), keys.astype(jnp.float32)) / jnp.sqrt(jnp.float32(HEAD))
    rows = lax.broadcasted_iota(jnp.int32, (SEQ, SEQ), 0)
    cols = lax.broadcasted_iota(jnp.int32, (SEQ, SEQ), 1)
    scores = jnp.where((cols <= rows)[None], scores, jnp.float32(-1e+30))
    top = lax.optimization_barrier(jnp.max(scores, axis=-1, keepdims=True))
    weights = jnp.exp(scores - top)
    probs = (weights / lax.optimization_barrier(jnp.sum(weights, axis=-1, keepdims=True))).astype(jnp.bfloat16)
    att = jnp.einsum('hqk,khd->qhd', probs.astype(jnp.float32), values.astype(jnp.float32)).reshape(SEQ, D)
    return (xf + value_g * att).astype(jnp.bfloat16)

def reference(acts, plan, norm_gain, query_gain, key_gain, value_gain):
    current = acts
    kept = []
    for step in range(STEPS):
        kept.append(jnp.roll(current, SECTIONS // 2, axis=0))
        laps = plan[step]

        def one_section(section_id):
            lap = laps[section_id]
            return mixer(current[section_id], norm_gain[section_id, lap], query_gain[section_id, lap], key_gain[section_id, lap], value_gain[section_id, lap])
        outputs = lax.map(one_section, jnp.arange(SECTIONS, dtype=jnp.int32))
        current = jnp.roll(outputs, 1, axis=0)
    return (current, jnp.stack(kept, axis=1))
```

```python
import functools
import math

import jax
import jax.numpy as jnp
from jax import lax
from jax.experimental import pallas as pl
from jax.experimental.pallas import tpu as pltpu
from jax.sharding import Mesh
from jax.sharding import PartitionSpec as P

D = 12288
HEAD = 128
BLOCK = 256
EPS = 1e-05
ACROSS_LAST = (((1,), (1,)), ((), ()))


def square_sums(y):
    yf = y.astype(jnp.float32)
    squared = yf * yf
    high = squared.astype(jnp.bfloat16)
    low = (squared - high.astype(jnp.float32)).astype(jnp.bfloat16)
    ones = jnp.ones((8, y.shape[1]), jnp.bfloat16)
    return lax.dot_general(ones, high, ACROSS_LAST, preferred_element_type=jnp.float32) + lax.dot_general(
        ones, low, ACROSS_LAST, preferred_element_type=jnp.float32
    )


def first_kernel(lap_ref, norm_ref, query_ref, key_ref, value_ref, x_ref, now_ref, later_ref):
    sums = square_sums(x_ref[...])
    rows = [[], []]
    for step in range(2):
        for gain in (norm_ref, query_ref, key_ref, value_ref):
            rows[step].append(jnp.where(lap_ref[step] == 0, gain[0:1], gain[1:2]))
    now_ref[...] = jnp.concatenate([sums[0:1]] + rows[0] + [sums[1:4]], axis=0)
    later_ref[...] = jnp.concatenate([sums[0:1]] + rows[1] + [sums[1:4]], axis=0)


def first(laps, gains, x):
    shape = jax.ShapeDtypeStruct((8, x.shape[1]), jnp.float32)
    return pl.pallas_call(
        first_kernel,
        in_specs=[pl.BlockSpec(memory_space=pltpu.SMEM)] + [pl.BlockSpec(memory_space=pltpu.VMEM)] * 5,
        out_shape=(shape, shape),
        compiler_params=pltpu.CompilerParams(vmem_limit_bytes=24 * 2**20),
    )(laps, *gains, x)


def mixer_kernel(with_sums, total_row, total_ref, gain_ref, x_ref, y_ref, *rest):
    seq, width = x_ref.shape
    scale = lax.rsqrt(total_ref[total_row : total_row + 1] / D + EPS)
    scale = jnp.transpose(jnp.broadcast_to(scale, (8, seq)))[:, 0:1]
    factor = math.log2(math.e) / math.sqrt(HEAD)
    causal = lax.broadcasted_iota(jnp.int32, (BLOCK, BLOCK), 1) <= lax.broadcasted_iota(
        jnp.int32, (BLOCK, BLOCK), 0
    )

    def prepare(head):
        cols = slice(head * HEAD, (head + 1) * HEAD)
        normed = x_ref[:, cols].astype(jnp.float32) * scale * gain_ref[1:2, cols]
        query = (normed * gain_ref[2:3, cols]).astype(jnp.bfloat16)
        keys = (normed * gain_ref[3:4, cols]).astype(jnp.bfloat16)
        return query, keys, normed.astype(jnp.bfloat16), cols

    def score(parts, block):
        query, keys, _, _ = parts
        lo, hi = block * BLOCK, (block + 1) * BLOCK
        raw = lax.dot_general(query[lo:hi], keys[:hi], ACROSS_LAST, preferred_element_type=jnp.float32)
        last = jnp.where(causal, raw[:, lo:], -1e30)
        return jnp.concatenate([raw[:, :lo], last], axis=1) if lo else last

    def softmax(raw):
        top = jnp.max(raw, axis=1, keepdims=True)
        weights = jnp.exp2((raw - top) * factor)
        return (weights * (1.0 / jnp.sum(weights, axis=1, keepdims=True))).astype(jnp.bfloat16)

    def finish(parts, block, probs):
        _, _, values, cols = parts
        lo, hi = block * BLOCK, (block + 1) * BLOCK
        att = jnp.dot(probs, values[:hi], preferred_element_type=jnp.float32)
        y_ref[lo:hi, cols] = (x_ref[lo:hi, cols].astype(jnp.float32) + gain_ref[4:5, cols] * att).astype(jnp.bfloat16)

    tasks = [(head, block) for head in range(width // HEAD) for block in range(seq // BLOCK)]
    ready = {}
    scores = {}

    def issue(at):
        head, block = tasks[at]
        if head not in ready:
            ready[head] = prepare(head)
        scores[at] = score(ready[head], block)

    issue(0)
    pending = None
    for at, (head, block) in enumerate(tasks):
        if at + 1 < len(tasks):
            issue(at + 1)
        probs = softmax(scores.pop(at))
        if pending is not None:
            finish(*pending)
        pending = (ready[head], block, probs)
    finish(*pending)
    if with_sums:
        rest[0][...] = square_sums(y_ref[...])


def mixer(x, total, row, gains, first_head=0, with_sums=False):
    seq, width = x.shape
    out_shape = [jax.ShapeDtypeStruct(x.shape, jnp.bfloat16)]
    out_specs = [pl.BlockSpec((seq, width), lambda i: (0, 0))]
    if with_sums:
        out_shape.append(jax.ShapeDtypeStruct((8, seq), jnp.float32))
        out_specs.append(pl.BlockSpec((8, seq), lambda i: (0, 0)))
    at = first_head * HEAD // width
    out = pl.pallas_call(
        functools.partial(mixer_kernel, with_sums, row),
        grid=(1,),
        in_specs=[
            pl.BlockSpec(total.shape, lambda i: (0, 0)),
            pl.BlockSpec((8, width), lambda i: (0, at)),
            pl.BlockSpec((seq, width), lambda i: (0, 0)),
        ],
        out_specs=out_specs,
        out_shape=out_shape,
        compiler_params=pltpu.CompilerParams(vmem_limit_bytes=32 * 2**20),
        cost_estimate=pl.CostEstimate(
            flops=12 * seq * seq * width, bytes_accessed=4 * seq * width, transcendentals=seq * seq * width // HEAD
        ),
    )(total, gains, x)
    return out if with_sums else out[0]


def moved(array, by):
    size = lax.axis_size("section")
    return lax.ppermute(array, "section", [(i, (i + by) % size) for i in range(size)])


def summed(part):
    size = lax.axis_size("z")
    copies = lax.all_to_all(jnp.broadcast_to(part[None], (size,) + part.shape), "z", 0, 0, tiled=True)
    return lax.psum(copies.sum(0), "xh")


def local(acts, plan, norm_gain, query_gain, key_gain, value_gain):
    half = lax.axis_size("section") // 2
    x = acts[0]
    width = x.shape[1] // 2
    laps = lax.dynamic_index_in_dim(plan, lax.axis_index("section"), 1, keepdims=False)
    now, later = first(laps, (norm_gain[0], query_gain[0], key_gain[0], value_gain[0]), x)
    gains_now = moved(now, 2)
    gains_mirror = moved(now, half)
    behind = moved(x, 2)
    mirror = [moved(x[:, i * width : (i + 1) * width], half) for i in range(2)]
    gains_later = moved(later, 1)

    totals = summed(jnp.concatenate([gains_now[0:1], gains_mirror[0:1]], axis=0))
    once, sums = mixer(behind, totals, 0, gains_now, with_sums=True)
    totals_later = summed(sums[0:1])
    early, totals_later = lax.optimization_barrier((mirror[0], totals_later))
    mixed = [mixer(early, totals, 1, gains_mirror)]
    twice = mixer(once, totals_later, 0, gains_later)
    late, twice = lax.optimization_barrier((mirror[1], twice))
    mixed.append(mixer(late, totals, 1, gains_mirror, first_head=width // HEAD))
    relayed = [moved(part, 1) for part in mixed]
    stash = jnp.stack([jnp.concatenate(mirror, axis=1), jnp.concatenate(relayed, axis=1)], axis=0)
    return (twice[None], stash[None])


def solution(mesh):
    sections, shards = mesh.shape["section"], mesh.shape["tp"]
    fine = Mesh(mesh.devices.reshape(sections, 2, shards // 2), ("section", "xh", "z"))
    tp = ("xh", "z")
    gain = P("section", None, tp)
    return jax.shard_map(
        local,
        mesh=fine,
        in_specs=(P("section", None, tp), P(), gain, gain, gain, gain),
        out_specs=(P("section", None, tp), P("section", None, None, tp)),
        check_vma=False,
    )
```

```python
import functools
import math

import jax
import jax.numpy as jnp
from jax import lax
from jax.experimental import pallas as pl
from jax.experimental.pallas import tpu as pltpu
from jax.sharding import Mesh
from jax.sharding import PartitionSpec as P

D = 12288
HEAD = 128
BLOCK = 256
EPS = 1e-05
ACROSS_LAST = (((1,), (1,)), ((), ()))
VMEM_LIMIT = 32 * 2**20
FREE = pl.CostEstimate(flops=0, bytes_accessed=0, transcendentals=0)


def square_sums(y):
    yf = y.astype(jnp.float32)
    squared = yf * yf
    high = squared.astype(jnp.bfloat16)
    low = (squared - high.astype(jnp.float32)).astype(jnp.bfloat16)
    ones = jnp.ones((8, y.shape[1]), jnp.bfloat16)
    return lax.dot_general(ones, high, ACROSS_LAST, preferred_element_type=jnp.float32) + lax.dot_general(
        ones, low, ACROSS_LAST, preferred_element_type=jnp.float32
    )


def first_kernel(lap_ref, norm_ref, query_ref, key_ref, value_ref, x_ref, sums_ref, now_ref, later_ref):
    sums_ref[...] = square_sums(x_ref[...])[0:1]
    for step, out_ref in enumerate((now_ref, later_ref)):
        for row, gain in enumerate((norm_ref, query_ref, key_ref, value_ref)):
            out_ref[row : row + 1] = jnp.where(lap_ref[step] == 0, gain[0:1], gain[1:2])


def first(laps, gains, x):
    width = x.shape[1]
    return pl.pallas_call(
        first_kernel,
        in_specs=[pl.BlockSpec(memory_space=pltpu.SMEM)] + [pl.BlockSpec(memory_space=pltpu.VMEM)] * 5,
        out_shape=(
            jax.ShapeDtypeStruct((1, x.shape[0]), jnp.float32),
            jax.ShapeDtypeStruct((4, width), jnp.float32),
            jax.ShapeDtypeStruct((4, width), jnp.float32),
        ),
        compiler_params=pltpu.CompilerParams(vmem_limit_bytes=60 * 2**20),
        cost_estimate=FREE,
    )(laps, *gains, x)


def mixer_kernel(with_sums, total_row, total_ref, gain_ref, x_ref, y_ref, *rest):
    seq, width = x_ref.shape
    scale = lax.rsqrt(total_ref[total_row : total_row + 1] / D + EPS)
    scale = jnp.transpose(jnp.broadcast_to(scale, (8, seq)))[:, 0:1]
    factor = math.log2(math.e) / math.sqrt(HEAD)
    causal = lax.broadcasted_iota(jnp.int32, (BLOCK, BLOCK), 1) <= lax.broadcasted_iota(
        jnp.int32, (BLOCK, BLOCK), 0
    )

    def prepare(head):
        cols = slice(head * HEAD, (head + 1) * HEAD)
        normed = x_ref[:, cols].astype(jnp.float32) * scale * gain_ref[0:1, cols]
        query = (normed * gain_ref[1:2, cols]).astype(jnp.bfloat16)
        keys = (normed * gain_ref[2:3, cols]).astype(jnp.bfloat16)
        return query, keys, normed.astype(jnp.bfloat16), cols

    def score(parts, block):
        query, keys, _, _ = parts
        lo, hi = block * BLOCK, (block + 1) * BLOCK
        raw = lax.dot_general(query[lo:hi], keys[:hi], ACROSS_LAST, preferred_element_type=jnp.float32)
        last = jnp.where(causal, raw[:, lo:], -1e30)
        return jnp.concatenate([raw[:, :lo], last], axis=1) if lo else last

    def softmax(raw):
        top = jnp.max(raw, axis=1, keepdims=True)
        weights = jnp.exp2((raw - top) * factor)
        return (weights * (1.0 / jnp.sum(weights, axis=1, keepdims=True))).astype(jnp.bfloat16)

    def finish(parts, block, probs):
        _, _, values, cols = parts
        lo, hi = block * BLOCK, (block + 1) * BLOCK
        att = jnp.dot(probs, values[:hi], preferred_element_type=jnp.float32)
        y_ref[lo:hi, cols] = (x_ref[lo:hi, cols].astype(jnp.float32) + gain_ref[3:4, cols] * att).astype(jnp.bfloat16)

    tasks = [(head, block) for head in range(width // HEAD) for block in range(seq // BLOCK)]
    ready = {}
    scores = {}

    def issue(at):
        head, block = tasks[at]
        if head not in ready:
            ready[head] = prepare(head)
        scores[at] = score(ready[head], block)

    issue(0)
    pending = None
    for at, (head, block) in enumerate(tasks):
        if at + 1 < len(tasks):
            issue(at + 1)
        probs = softmax(scores.pop(at))
        if pending is not None:
            finish(*pending)
        pending = (ready[head], block, probs)
    finish(*pending)
    if with_sums:
        rest[0][...] = square_sums(y_ref[...])


def mixer(x, total, row, gains, first_head=0, with_sums=False, cost=0):
    seq, width = x.shape
    out_shape = [jax.ShapeDtypeStruct(x.shape, jnp.bfloat16)]
    out_specs = [pl.BlockSpec((seq, width), lambda i: (0, 0))]
    if with_sums:
        out_shape.append(jax.ShapeDtypeStruct((8, seq), jnp.float32))
        out_specs.append(pl.BlockSpec((8, seq), lambda i: (0, 0)))
    at = first_head * HEAD // width
    out = pl.pallas_call(
        functools.partial(mixer_kernel, with_sums, row),
        grid=(1,),
        in_specs=[
            pl.BlockSpec(total.shape, lambda i: (0, 0)),
            pl.BlockSpec((gains.shape[0], width), lambda i: (0, at)),
            pl.BlockSpec((seq, width), lambda i: (0, 0)),
        ],
        out_specs=out_specs,
        out_shape=out_shape,
        compiler_params=pltpu.CompilerParams(vmem_limit_bytes=VMEM_LIMIT),
        cost_estimate=pl.CostEstimate(flops=cost, bytes_accessed=0, transcendentals=0),
    )(total, gains, x)
    return out if with_sums else out[0]


def moved(array, by):
    size = lax.axis_size("section")
    return lax.ppermute(array, "section", [(i, (i + by) % size) for i in range(size)])


def summed(part):
    size = lax.axis_size("z")
    copies = lax.all_to_all(jnp.broadcast_to(part[None], (size,) + part.shape), "z", 0, 0, tiled=True)
    return lax.psum(copies.sum(0), "xh")


def local(acts, plan, norm_gain, query_gain, key_gain, value_gain):
    half = lax.axis_size("section") // 2
    x = acts[0]
    width = x.shape[1] // 2
    laps = lax.dynamic_index_in_dim(plan, lax.axis_index("section"), 1, keepdims=False)
    mirror = [moved(x[:, i * width : (i + 1) * width], half) for i in range(2)]
    behind = moved(x, 2)
    sums, now, later = first(laps, (norm_gain[0], query_gain[0], key_gain[0], value_gain[0]), x)
    gains_later = moved(later, 1)
    packet = jnp.concatenate([now, summed(sums)], axis=0)
    packet, gains_later = lax.optimization_barrier((packet, gains_later))
    behind_packet = moved(packet, 2)
    mirror_packet = moved(packet, half)

    once, sums = mixer(behind, behind_packet, 4, behind_packet, with_sums=True)
    total = summed(sums[0:1])
    chunk, total = lax.optimization_barrier((mirror[0], total))
    first_part = mixer(chunk, mirror_packet, 4, mirror_packet)
    chunk, first_part = lax.optimization_barrier((mirror[1], first_part))
    second_part = mixer(chunk, mirror_packet, 4, mirror_packet, first_head=width // HEAD, cost=10**10)
    relayed = [moved(first_part, 1), moved(second_part, 1)]
    total, second_part = lax.optimization_barrier((total, second_part))
    twice = mixer(once, total, 0, gains_later)
    stash = jnp.stack([jnp.concatenate(mirror, axis=1), jnp.concatenate(relayed, axis=1)], axis=0)
    return (twice[None], stash[None])


def solution(mesh):
    sections, shards = mesh.shape["section"], mesh.shape["tp"]
    fine = Mesh(mesh.devices.reshape(sections, 2, shards // 2), ("section", "xh", "z"))
    tp = ("xh", "z")
    gain = P("section", None, tp)
    return jax.shard_map(
        local,
        mesh=fine,
        in_specs=(P("section", None, tp), P(), gain, gain, gain, gain),
        out_specs=(P("section", None, tp), P("section", None, None, tp)),
        check_vma=False,
    )
```

```python
import functools
import math

import jax
import jax.numpy as jnp
from jax import lax
from jax.experimental import pallas as pl
from jax.experimental.pallas import tpu as pltpu
from jax.sharding import Mesh
from jax.sharding import PartitionSpec as P

D = 12288
HEAD = 128
BLOCK = 256
EPS = 1e-05
FAR = (512, 256)
TAIL = 32
ACROSS_LAST = (((1,), (1,)), ((), ()))
VMEM_LIMIT = 32 * 2**20
FREE = pl.CostEstimate(flops=0, bytes_accessed=0, transcendentals=0)


def square_sums(y):
    yf = y.astype(jnp.float32)
    squared = yf * yf
    high = squared.astype(jnp.bfloat16)
    low = (squared - high.astype(jnp.float32)).astype(jnp.bfloat16)
    ones = jnp.ones((8, y.shape[1]), jnp.bfloat16)
    sums = lax.dot_general(ones, high, ACROSS_LAST, preferred_element_type=jnp.float32) + lax.dot_general(
        ones, low, ACROSS_LAST, preferred_element_type=jnp.float32
    )
    return sums[0:1]


def thirds(value):
    high = value.astype(jnp.bfloat16).astype(jnp.float32)
    middle = (value - high).astype(jnp.bfloat16).astype(jnp.float32)
    return [high, middle, value - high - middle]


def chosen(plan_ref, step, gains):
    lap = plan_ref[step, lax.axis_index("section")]
    return jnp.concatenate([jnp.where(lap == 0, gain[0:1], gain[1:2]) for gain in gains], axis=0)


def first_kernel(plan_ref, norm_ref, query_ref, key_ref, value_ref, x_ref, now_ref, later_ref, sums_ref):
    gains = (norm_ref, query_ref, key_ref, value_ref)
    now_ref[...] = chosen(plan_ref, 0, gains)
    later_ref[...] = chosen(plan_ref, 1, gains)
    sums = square_sums(x_ref[...])
    for copy in range(sums_ref.shape[0]):
        sums_ref[copy] = sums


def first(plan, gains, x, copies):
    seq, width = x.shape
    gain = jax.ShapeDtypeStruct((4, width), jnp.float32)
    return pl.pallas_call(
        first_kernel,
        in_specs=[pl.BlockSpec(memory_space=pltpu.SMEM)] + [pl.BlockSpec(memory_space=pltpu.VMEM)] * 5,
        out_shape=(gain, gain, jax.ShapeDtypeStruct((copies, 1, seq), jnp.float32)),
        compiler_params=pltpu.CompilerParams(vmem_limit_bytes=60 * 2**20),
        cost_estimate=FREE,
    )(plan, *gains, x)


def rows_of(value, width):
    count = -(-value.shape[1] // width)
    rest = count * width - value.shape[1]
    if rest:
        value = jnp.concatenate([value, jnp.zeros((1, rest), value.dtype)], axis=1)
    return [value[:, at * width : (at + 1) * width] for at in range(count)]


def pack_kernel(total_ref, now_ref, x_ref, packet_ref, *part_refs):
    seq = x_ref.shape[0]
    packet_ref[0:4] = now_ref[...]
    packet_ref[4:5] = total_ref[...]
    col = 0
    for part_ref in part_refs:
        part = part_ref.shape[1]
        cols = slice(col, col + part)
        part_ref[:seq] = x_ref[:, cols]
        tail = thirds(now_ref[:, cols])
        for third in thirds(total_ref[...]):
            tail += rows_of(third, part)
        used = sum(rows.shape[0] for rows in tail)
        tail = jnp.concatenate(tail + [jnp.zeros((TAIL - used, part), jnp.float32)], axis=0)
        part_ref[seq:] = tail.astype(jnp.bfloat16)
        col += part


def packed(total, now, x):
    seq, width = x.shape
    parts = tuple(jax.ShapeDtypeStruct((seq + TAIL, part), jnp.bfloat16) for part in FAR)
    return pl.pallas_call(
        pack_kernel,
        out_shape=(jax.ShapeDtypeStruct((5, width), jnp.float32),) + parts,
        compiler_params=pltpu.CompilerParams(vmem_limit_bytes=VMEM_LIMIT),
        cost_estimate=FREE,
    )(total, now, x)


def unpacked(part_ref, seq):
    tail = part_ref[seq:].astype(jnp.float32)
    gains = tail[0:4] + tail[4:8] + tail[8:12]
    count = -(-seq // part_ref.shape[1])
    rows = tail[12 : 12 + count] + tail[12 + count : 12 + 2 * count] + tail[12 + 2 * count : 12 + 3 * count]
    return gains, jnp.concatenate([rows[at : at + 1] for at in range(count)], axis=1)[:, :seq]


def mixer_kernel(config, x_ref, *refs):
    plain, row, with_sums = config
    if plain:
        total_ref, gain_ref, y_ref, rest = refs[0], refs[1], refs[2], refs[3:]
        total, gain = total_ref[row : row + 1], gain_ref[...]
    else:
        y_ref, rest = refs[0], refs[1:]
        gain, total = unpacked(x_ref, y_ref.shape[0])
    seq, width = y_ref.shape
    scale = lax.rsqrt(total / D + EPS)
    scale = jnp.transpose(jnp.broadcast_to(scale, (8, seq)))[:, 0:1]
    factor = math.log2(math.e) / math.sqrt(HEAD)
    causal = lax.broadcasted_iota(jnp.int32, (BLOCK, BLOCK), 1) <= lax.broadcasted_iota(
        jnp.int32, (BLOCK, BLOCK), 0
    )

    def prepare(head):
        cols = slice(head * HEAD, (head + 1) * HEAD)
        normed = x_ref[:seq, cols].astype(jnp.float32) * scale * gain[0:1, cols]
        query = (normed * gain[1:2, cols]).astype(jnp.bfloat16)
        keys = (normed * gain[2:3, cols]).astype(jnp.bfloat16)
        return query, keys, normed.astype(jnp.bfloat16), gain[3:4, cols], cols

    def score(ready, block):
        query, keys = ready[:2]
        lo, hi = block * BLOCK, (block + 1) * BLOCK
        raw = lax.dot_general(query[lo:hi], keys[:hi], ACROSS_LAST, preferred_element_type=jnp.float32)
        last = jnp.where(causal, raw[:, lo:], -1e30)
        return jnp.concatenate([raw[:, :lo], last], axis=1) if lo else last

    def softmax(raw):
        top = jnp.max(raw, axis=1, keepdims=True)
        weights = jnp.exp2((raw - top) * factor)
        return (weights * (1.0 / jnp.sum(weights, axis=1, keepdims=True))).astype(jnp.bfloat16)

    def finish(ready, block, probs):
        values, value_gain, cols = ready[2:]
        lo, hi = block * BLOCK, (block + 1) * BLOCK
        att = jnp.dot(probs, values[:hi], preferred_element_type=jnp.float32)
        y_ref[lo:hi, cols] = (
            x_ref[lo:hi, cols].astype(jnp.float32) + value_gain * att
        ).astype(jnp.bfloat16)

    tasks = [(head, block) for head in range(width // HEAD) for block in range(seq // BLOCK)]
    prepared = {}
    scores = {}

    def issue(at):
        head, block = tasks[at]
        if head not in prepared:
            prepared[head] = prepare(head)
        scores[at] = score(prepared[head], block)

    issue(0)
    pending = None
    for at, (head, block) in enumerate(tasks):
        if at + 1 < len(tasks):
            issue(at + 1)
        probs = softmax(scores.pop(at))
        if pending is not None:
            finish(*pending)
        pending = (prepared[head], block, probs)
    finish(*pending)
    if with_sums:
        sums = square_sums(y_ref[...])
        for copy in range(rest[0].shape[0]):
            rest[0][copy] = sums


def mixer(x, seq, total=None, row=0, gains=None, copies=0):
    width = x.shape[1]
    out_shape = [jax.ShapeDtypeStruct((seq, width), jnp.bfloat16)]
    if copies:
        out_shape.append(jax.ShapeDtypeStruct((copies, 1, seq), jnp.float32))
    plain = total is not None
    operands = (x, total, gains) if plain else (x,)
    whole = lambda array: pl.BlockSpec(array.shape, lambda i: (0,) * len(array.shape))
    out = pl.pallas_call(
        functools.partial(mixer_kernel, (plain, row, copies > 0)),
        grid=(1,),
        in_specs=[whole(operand) for operand in operands],
        out_specs=[whole(shape) for shape in out_shape],
        out_shape=out_shape,
        compiler_params=pltpu.CompilerParams(vmem_limit_bytes=VMEM_LIMIT),
        cost_estimate=FREE,
    )(*operands)
    return out if copies else out[0]


def place_kernel(*refs):
    out_ref = refs[-1]
    seq = out_ref.shape[1]
    slot, col = 0, 0
    for ref in refs[:-1]:
        out_ref[slot, :, col : col + ref.shape[1]] = ref[:seq]
        col += ref.shape[1]
        if col == out_ref.shape[2]:
            slot, col = slot + 1, 0


def place(parts, shape):
    return pl.pallas_call(
        place_kernel,
        in_specs=[pl.BlockSpec(memory_space=pltpu.VMEM)] * len(parts),
        out_specs=pl.BlockSpec(memory_space=pltpu.VMEM),
        out_shape=jax.ShapeDtypeStruct(shape, jnp.bfloat16),
        compiler_params=pltpu.CompilerParams(vmem_limit_bytes=VMEM_LIMIT),
        cost_estimate=FREE,
    )(*parts)


def moved(array, target):
    size = lax.axis_size("section")
    return lax.ppermute(array, "section", [(i, target(i) % size) for i in range(size)])


def summed(copies):
    return lax.psum(lax.all_to_all(copies, "z", 0, 0, tiled=True).sum(0), "xh")


def local(acts, plan, norm_gain, query_gain, key_gain, value_gain):
    half = lax.axis_size("section") // 2
    along = lax.axis_size("z")
    x = acts[0]
    seq, width = x.shape
    gains = (norm_gain[0], query_gain[0], key_gain[0], value_gain[0])
    behind = moved(x, lambda s: s + 2)
    now, later, copies = first(plan, gains, x, along)
    gains_later = moved(later, lambda s: s + 1)
    packet, far_left, far_right = packed(summed(copies), now, x)
    packet = moved(packet, lambda s: s + 2)
    far_left, far_right, behind, packet, gains_later = lax.optimization_barrier(
        (far_left, far_right, behind, packet, gains_later)
    )
    mirror_left = moved(far_left, lambda s: s + half)
    mirror_right = moved(far_right, lambda s: s + half)

    once, copies = mixer(behind, seq, packet, 4, packet, copies=along)
    twice = mixer(once, seq, summed(copies), 0, gains_later)
    mirror_left, twice = lax.optimization_barrier((mirror_left, twice))
    left = mixer(mirror_left, seq)
    mirror_right, left = lax.optimization_barrier((mirror_right, left))
    right = mixer(mirror_right, seq)
    left = moved(left, lambda s: s + 1)
    right = moved(right, lambda s: s + 1)
    stash = place([mirror_left, mirror_right, left], (2, seq, width))
    stash = lax.dynamic_update_slice(stash, right[None], (1, 0, FAR[0]))
    return (twice[None], stash[None])


def solution(mesh):
    sections, shards = mesh.shape["section"], mesh.shape["tp"]
    fine = Mesh(mesh.devices.reshape(sections, 2, shards // 2), ("section", "xh", "z"))
    tp = ("xh", "z")
    gain = P("section", None, tp)
    return jax.shard_map(
        local,
        mesh=fine,
        in_specs=(P("section", None, tp), P(), gain, gain, gain, gain),
        out_specs=(P("section", None, tp), P("section", None, None, tp)),
        check_vma=False,
    )
```

```python
import functools
import math

import jax
import jax.numpy as jnp
from jax import lax
from jax.experimental import pallas as pl
from jax.experimental.pallas import tpu as pltpu
from jax.sharding import Mesh
from jax.sharding import PartitionSpec as P

D = 12288
HEAD = 128
BLOCK = 256
EPS = 1e-05
FAR = (512, 256)
TAIL = 32
ACROSS_LAST = (((1,), (1,)), ((), ()))
VMEM_LIMIT = 32 * 2**20
FREE = pl.CostEstimate(flops=0, bytes_accessed=0, transcendentals=0)


def square_sums(y):
    yf = y.astype(jnp.float32)
    squared = yf * yf
    high = squared.astype(jnp.bfloat16)
    low = (squared - high.astype(jnp.float32)).astype(jnp.bfloat16)
    ones = jnp.ones((8, y.shape[1]), jnp.bfloat16)
    sums = lax.dot_general(ones, high, ACROSS_LAST, preferred_element_type=jnp.float32) + lax.dot_general(
        ones, low, ACROSS_LAST, preferred_element_type=jnp.float32
    )
    return sums[0:1]


def thirds(value):
    high = value.astype(jnp.bfloat16).astype(jnp.float32)
    middle = (value - high).astype(jnp.bfloat16).astype(jnp.float32)
    return [high, middle, value - high - middle]


def chosen(plan_ref, step, gains):
    lap = plan_ref[step, lax.axis_index("section")]
    return jnp.concatenate([jnp.where(lap == 0, gain[0:1], gain[1:2]) for gain in gains], axis=0)


def first_kernel(plan_ref, norm_ref, query_ref, key_ref, value_ref, x_ref, now_ref, later_ref, sums_ref, *part_refs):
    seq = x_ref.shape[0]
    gains = (norm_ref, query_ref, key_ref, value_ref)
    now = chosen(plan_ref, 0, gains)
    now_ref[...] = now
    sums = square_sums(x_ref[...])
    for copy in range(sums_ref.shape[0]):
        sums_ref[copy] = sums
    later_ref[...] = chosen(plan_ref, 1, gains)
    col = 0
    for part_ref in part_refs:
        part = part_ref.shape[1]
        cols = slice(col, col + part)
        part_ref[:seq] = x_ref[:, cols]
        tail = thirds(now[:, cols]) + [jnp.zeros((TAIL - 12, part), jnp.float32)]
        part_ref[seq:] = jnp.concatenate(tail, axis=0).astype(jnp.bfloat16)
        col += part


def first(plan, gains, x, copies):
    seq, width = x.shape
    gain = jax.ShapeDtypeStruct((4, width), jnp.float32)
    parts = tuple(jax.ShapeDtypeStruct((seq + TAIL, part), jnp.bfloat16) for part in FAR)
    return pl.pallas_call(
        first_kernel,
        in_specs=[pl.BlockSpec(memory_space=pltpu.SMEM)] + [pl.BlockSpec(memory_space=pltpu.VMEM)] * 5,
        out_shape=(gain, gain, jax.ShapeDtypeStruct((copies, 1, seq), jnp.float32)) + parts,
        compiler_params=pltpu.CompilerParams(vmem_limit_bytes=60 * 2**20),
        cost_estimate=FREE,
    )(plan, *gains, x)


def rows_of(value, width):
    count = -(-value.shape[1] // width)
    rest = count * width - value.shape[1]
    if rest:
        value = jnp.concatenate([value, jnp.zeros((1, rest), value.dtype)], axis=1)
    return [value[:, at * width : (at + 1) * width] for at in range(count)]


def pack_kernel(total_ref, now_ref, *refs):
    count = len(refs) // 2
    packet_ref = refs[count]
    packet_ref[0:4] = now_ref[...]
    packet_ref[4:5] = total_ref[...]
    for tail_ref, out_ref in zip(refs[:count], refs[count + 1 :]):
        part = out_ref.shape[1]
        rows = [piece for third in thirds(total_ref[...]) for piece in rows_of(third, part)]
        used = 12 + len(rows)
        tail = [tail_ref[0:12].astype(jnp.float32)] + rows + [jnp.zeros((TAIL - used, part), jnp.float32)]
        out_ref[...] = jnp.concatenate(tail, axis=0).astype(jnp.bfloat16)


def packed(total, now, parts):
    specs = [pl.BlockSpec((TAIL, part.shape[1]), lambda i, at=part.shape[0] // TAIL - 1: (at, 0)) for part in parts]
    whole = lambda shape: pl.BlockSpec(shape, lambda i: (0, 0))
    packet = (5, now.shape[1])
    return pl.pallas_call(
        pack_kernel,
        grid=(1,),
        in_specs=[whole(total.shape), whole(now.shape)] + specs,
        out_specs=[whole(packet)] + specs,
        out_shape=[jax.ShapeDtypeStruct(packet, jnp.float32)]
        + [jax.ShapeDtypeStruct(part.shape, part.dtype) for part in parts],
        input_output_aliases={2 + at: 1 + at for at in range(len(parts))},
        compiler_params=pltpu.CompilerParams(vmem_limit_bytes=60 * 2**20),
        cost_estimate=FREE,
    )(total, now, *parts)


def unpacked(part_ref, seq):
    tail = part_ref[seq:].astype(jnp.float32)
    gains = tail[0:4] + tail[4:8] + tail[8:12]
    count = -(-seq // part_ref.shape[1])
    rows = tail[12 : 12 + count] + tail[12 + count : 12 + 2 * count] + tail[12 + 2 * count : 12 + 3 * count]
    return gains, jnp.concatenate([rows[at : at + 1] for at in range(count)], axis=1)[:, :seq]


def mixer_kernel(config, x_ref, *refs):
    plain, row, with_sums = config
    if plain:
        total_ref, gain_ref, y_ref, rest = refs[0], refs[1], refs[2], refs[3:]
        total, gain = total_ref[row : row + 1], gain_ref[...]
    else:
        y_ref, rest = refs[0], refs[1:]
        gain, total = unpacked(x_ref, y_ref.shape[0])
    seq, width = y_ref.shape
    scale = lax.rsqrt(total / D + EPS)
    scale = jnp.transpose(jnp.broadcast_to(scale, (8, seq)))[:, 0:1]
    factor = math.log2(math.e) / math.sqrt(HEAD)
    causal = lax.broadcasted_iota(jnp.int32, (BLOCK, BLOCK), 1) <= lax.broadcasted_iota(
        jnp.int32, (BLOCK, BLOCK), 0
    )

    def prepare(head):
        cols = slice(head * HEAD, (head + 1) * HEAD)
        normed = x_ref[:seq, cols].astype(jnp.float32) * scale * gain[0:1, cols]
        query = (normed * gain[1:2, cols]).astype(jnp.bfloat16)
        keys = (normed * gain[2:3, cols]).astype(jnp.bfloat16)
        return query, keys, normed.astype(jnp.bfloat16), gain[3:4, cols], cols

    def score(ready, block):
        query, keys = ready[:2]
        lo, hi = block * BLOCK, (block + 1) * BLOCK
        raw = lax.dot_general(query[lo:hi], keys[:hi], ACROSS_LAST, preferred_element_type=jnp.float32)
        last = jnp.where(causal, raw[:, lo:], -1e30)
        return jnp.concatenate([raw[:, :lo], last], axis=1) if lo else last

    def softmax(raw):
        top = jnp.max(raw, axis=1, keepdims=True)
        weights = jnp.exp2((raw - top) * factor)
        return (weights * (1.0 / jnp.sum(weights, axis=1, keepdims=True))).astype(jnp.bfloat16)

    def finish(ready, block, probs):
        values, value_gain, cols = ready[2:]
        lo, hi = block * BLOCK, (block + 1) * BLOCK
        att = jnp.dot(probs, values[:hi], preferred_element_type=jnp.float32)
        y_ref[lo:hi, cols] = (
            x_ref[lo:hi, cols].astype(jnp.float32) + value_gain * att
        ).astype(jnp.bfloat16)

    tasks = [(head, block) for head in range(width // HEAD) for block in range(seq // BLOCK)]
    prepared = {}
    scores = {}

    def issue(at):
        head, block = tasks[at]
        if head not in prepared:
            prepared[head] = prepare(head)
        scores[at] = score(prepared[head], block)

    issue(0)
    pending = None
    for at, (head, block) in enumerate(tasks):
        if at + 1 < len(tasks):
            issue(at + 1)
        probs = softmax(scores.pop(at))
        if pending is not None:
            finish(*pending)
        pending = (prepared[head], block, probs)
    finish(*pending)
    if with_sums:
        sums = square_sums(y_ref[...])
        for copy in range(rest[0].shape[0]):
            rest[0][copy] = sums


def mixer(x, seq, total=None, row=0, gains=None, copies=0):
    width = x.shape[1]
    out_shape = [jax.ShapeDtypeStruct((seq, width), jnp.bfloat16)]
    if copies:
        out_shape.append(jax.ShapeDtypeStruct((copies, 1, seq), jnp.float32))
    plain = total is not None
    operands = (x, total, gains) if plain else (x,)
    whole = lambda array: pl.BlockSpec(array.shape, lambda i: (0,) * len(array.shape))
    out = pl.pallas_call(
        functools.partial(mixer_kernel, (plain, row, copies > 0)),
        grid=(1,),
        in_specs=[whole(operand) for operand in operands],
        out_specs=[whole(shape) for shape in out_shape],
        out_shape=out_shape,
        compiler_params=pltpu.CompilerParams(vmem_limit_bytes=VMEM_LIMIT),
        cost_estimate=FREE,
    )(*operands)
    return out if copies else out[0]


def place_kernel(*refs):
    out_ref = refs[-1]
    seq = out_ref.shape[1]
    slot, col = 0, 0
    for ref in refs[:-1]:
        out_ref[slot, :, col : col + ref.shape[1]] = ref[:seq]
        col += ref.shape[1]
        if col == out_ref.shape[2]:
            slot, col = slot + 1, 0


def place(parts, shape):
    return pl.pallas_call(
        place_kernel,
        in_specs=[pl.BlockSpec(memory_space=pltpu.VMEM)] * len(parts),
        out_specs=pl.BlockSpec(memory_space=pltpu.VMEM),
        out_shape=jax.ShapeDtypeStruct(shape, jnp.bfloat16),
        compiler_params=pltpu.CompilerParams(vmem_limit_bytes=VMEM_LIMIT),
        cost_estimate=FREE,
    )(*parts)


def moved(array, target):
    size = lax.axis_size("section")
    return lax.ppermute(array, "section", [(i, target(i) % size) for i in range(size)])


def summed(copies):
    return lax.psum(lax.all_to_all(copies, "z", 0, 0, tiled=True).sum(0), "xh")


def local(acts, plan, norm_gain, query_gain, key_gain, value_gain):
    half = lax.axis_size("section") // 2
    along = lax.axis_size("z")
    x = acts[0]
    seq, width = x.shape
    gains = (norm_gain[0], query_gain[0], key_gain[0], value_gain[0])
    behind = moved(x, lambda s: s + 2)
    now, later, copies, *parts = first(plan, gains, x, along)
    gains_later = moved(later, lambda s: s + 1)
    total, gains_later = lax.optimization_barrier((summed(copies), gains_later))
    packet, far_left, far_right = packed(total, now, parts)
    packet = moved(packet, lambda s: s + 2)
    far_left, far_right, behind, packet = lax.optimization_barrier((far_left, far_right, behind, packet))
    mirror_left = moved(far_left, lambda s: s + half)

    once, copies = mixer(behind, seq, packet, 4, packet, copies=along)
    mirror_right = moved(far_right, lambda s: s + half)
    twice = mixer(once, seq, summed(copies), 0, gains_later)
    mirror_left, twice = lax.optimization_barrier((mirror_left, twice))
    left = mixer(mirror_left, seq)
    mirror_right, _ = lax.optimization_barrier((mirror_right, left))
    right = mixer(mirror_right, seq)
    left = moved(left, lambda s: s + 1)
    right = moved(right, lambda s: s + 1)
    stash = place([mirror_left, mirror_right, left], (2, seq, width))
    stash = lax.dynamic_update_slice(stash, right[None], (1, 0, FAR[0]))
    return (twice[None], stash[None])


def solution(mesh):
    sections, shards = mesh.shape["section"], mesh.shape["tp"]
    fine = Mesh(mesh.devices.reshape(sections, 2, shards // 2), ("section", "xh", "z"))
    tp = ("xh", "z")
    gain = P("section", None, tp)
    return jax.shard_map(
        local,
        mesh=fine,
        in_specs=(P("section", None, tp), P(), gain, gain, gain, gain),
        out_specs=(P("section", None, tp), P("section", None, None, tp)),
        check_vma=False,
    )
```

```python
import functools
import math

import jax
import jax.numpy as jnp
from jax import lax
from jax.experimental import pallas as pl
from jax.experimental.pallas import tpu as pltpu
from jax.sharding import Mesh
from jax.sharding import PartitionSpec as P

D = 12288
HEAD = 128
BLOCK = 256
EPS = 1e-05
FAR = (256, 256, 256)
TAIL = 32
ACROSS_LAST = (((1,), (1,)), ((), ()))
VMEM_LIMIT = 32 * 2**20
FREE = pl.CostEstimate(flops=0, bytes_accessed=0, transcendentals=0)


def square_sums(y):
    yf = y.astype(jnp.float32)
    squared = yf * yf
    high = squared.astype(jnp.bfloat16)
    low = (squared - high.astype(jnp.float32)).astype(jnp.bfloat16)
    ones = jnp.ones((8, y.shape[1]), jnp.bfloat16)
    sums = lax.dot_general(ones, high, ACROSS_LAST, preferred_element_type=jnp.float32) + lax.dot_general(
        ones, low, ACROSS_LAST, preferred_element_type=jnp.float32
    )
    return sums[0:1]


def thirds(value):
    high = value.astype(jnp.bfloat16).astype(jnp.float32)
    middle = (value - high).astype(jnp.bfloat16).astype(jnp.float32)
    return [high, middle, value - high - middle]


def chosen(plan_ref, step, gains):
    lap = plan_ref[step, lax.axis_index("section")]
    return jnp.concatenate([jnp.where(lap == 0, gain[0:1], gain[1:2]) for gain in gains], axis=0)


def first_kernel(plan_ref, norm_ref, query_ref, key_ref, value_ref, x_ref, now_ref, later_ref, sums_ref, *part_refs):
    seq = x_ref.shape[0]
    gains = (norm_ref, query_ref, key_ref, value_ref)
    now = chosen(plan_ref, 0, gains)
    now_ref[...] = now
    sums = square_sums(x_ref[...])
    for copy in range(sums_ref.shape[0]):
        sums_ref[copy] = sums
    later_ref[...] = chosen(plan_ref, 1, gains)
    col = 0
    for part_ref in part_refs:
        part = part_ref.shape[1]
        cols = slice(col, col + part)
        part_ref[:seq] = x_ref[:, cols]
        tail = thirds(now[:, cols]) + [jnp.zeros((TAIL - 12, part), jnp.float32)]
        part_ref[seq:] = jnp.concatenate(tail, axis=0).astype(jnp.bfloat16)
        col += part


def first(plan, gains, x, copies):
    seq, width = x.shape
    gain = jax.ShapeDtypeStruct((4, width), jnp.float32)
    parts = tuple(jax.ShapeDtypeStruct((seq + TAIL, part), jnp.bfloat16) for part in FAR)
    return pl.pallas_call(
        first_kernel,
        in_specs=[pl.BlockSpec(memory_space=pltpu.SMEM)] + [pl.BlockSpec(memory_space=pltpu.VMEM)] * 5,
        out_shape=(gain, gain, jax.ShapeDtypeStruct((copies, 1, seq), jnp.float32)) + parts,
        compiler_params=pltpu.CompilerParams(vmem_limit_bytes=60 * 2**20),
        cost_estimate=FREE,
    )(plan, *gains, x)


def rows_of(value, width):
    count = -(-value.shape[1] // width)
    rest = count * width - value.shape[1]
    if rest:
        value = jnp.concatenate([value, jnp.zeros((1, rest), value.dtype)], axis=1)
    return [value[:, at * width : (at + 1) * width] for at in range(count)]


def pack_kernel(total_ref, now_ref, *refs):
    count = len(refs) // 2
    packet_ref = refs[count]
    packet_ref[0:4] = now_ref[...]
    packet_ref[4:5] = total_ref[...]
    for tail_ref, out_ref in zip(refs[:count], refs[count + 1 :]):
        part = out_ref.shape[1]
        rows = [piece for third in thirds(total_ref[...]) for piece in rows_of(third, part)]
        used = 12 + len(rows)
        tail = [tail_ref[0:12].astype(jnp.float32)] + rows + [jnp.zeros((TAIL - used, part), jnp.float32)]
        out_ref[...] = jnp.concatenate(tail, axis=0).astype(jnp.bfloat16)


def packed(total, now, parts):
    specs = [pl.BlockSpec((TAIL, part.shape[1]), lambda i, at=part.shape[0] // TAIL - 1: (at, 0)) for part in parts]
    whole = lambda shape: pl.BlockSpec(shape, lambda i: (0, 0))
    packet = (5, now.shape[1])
    return pl.pallas_call(
        pack_kernel,
        grid=(1,),
        in_specs=[whole(total.shape), whole(now.shape)] + specs,
        out_specs=[whole(packet)] + specs,
        out_shape=[jax.ShapeDtypeStruct(packet, jnp.float32)]
        + [jax.ShapeDtypeStruct(part.shape, part.dtype) for part in parts],
        input_output_aliases={2 + at: 1 + at for at in range(len(parts))},
        compiler_params=pltpu.CompilerParams(vmem_limit_bytes=60 * 2**20),
        cost_estimate=FREE,
    )(total, now, *parts)


def unpacked(part_ref, seq):
    tail = part_ref[seq:].astype(jnp.float32)
    gains = tail[0:4] + tail[4:8] + tail[8:12]
    count = -(-seq // part_ref.shape[1])
    rows = tail[12 : 12 + count] + tail[12 + count : 12 + 2 * count] + tail[12 + 2 * count : 12 + 3 * count]
    return gains, jnp.concatenate([rows[at : at + 1] for at in range(count)], axis=1)[:, :seq]


def mixer_kernel(config, x_ref, *refs):
    plain, row, with_sums = config
    if plain:
        total_ref, gain_ref, y_ref, rest = refs[0], refs[1], refs[2], refs[3:]
        total, gain = total_ref[row : row + 1], gain_ref[...]
    else:
        y_ref, rest = refs[0], refs[1:]
        gain, total = unpacked(x_ref, y_ref.shape[0])
    seq, width = y_ref.shape
    scale = lax.rsqrt(total / D + EPS)
    scale = jnp.transpose(jnp.broadcast_to(scale, (8, seq)))[:, 0:1]
    factor = math.log2(math.e) / math.sqrt(HEAD)
    causal = lax.broadcasted_iota(jnp.int32, (BLOCK, BLOCK), 1) <= lax.broadcasted_iota(
        jnp.int32, (BLOCK, BLOCK), 0
    )

    def prepare(head):
        cols = slice(head * HEAD, (head + 1) * HEAD)
        normed = x_ref[:seq, cols].astype(jnp.float32) * scale * gain[0:1, cols]
        query = (normed * gain[1:2, cols]).astype(jnp.bfloat16)
        keys = (normed * gain[2:3, cols]).astype(jnp.bfloat16)
        return query, keys, normed.astype(jnp.bfloat16), gain[3:4, cols], cols

    def score(ready, block):
        query, keys = ready[:2]
        lo, hi = block * BLOCK, (block + 1) * BLOCK
        raw = lax.dot_general(query[lo:hi], keys[:hi], ACROSS_LAST, preferred_element_type=jnp.float32)
        last = jnp.where(causal, raw[:, lo:], -1e30)
        return jnp.concatenate([raw[:, :lo], last], axis=1) if lo else last

    def softmax(raw):
        top = jnp.max(raw, axis=1, keepdims=True)
        weights = jnp.exp2((raw - top) * factor)
        return (weights * (1.0 / jnp.sum(weights, axis=1, keepdims=True))).astype(jnp.bfloat16)

    def finish(ready, block, probs):
        values, value_gain, cols = ready[2:]
        lo, hi = block * BLOCK, (block + 1) * BLOCK
        att = jnp.dot(probs, values[:hi], preferred_element_type=jnp.float32)
        y_ref[lo:hi, cols] = (
            x_ref[lo:hi, cols].astype(jnp.float32) + value_gain * att
        ).astype(jnp.bfloat16)

    tasks = [(head, block) for head in range(width // HEAD) for block in range(seq // BLOCK)]
    prepared = {}
    scores = {}

    def issue(at):
        head, block = tasks[at]
        if head not in prepared:
            prepared[head] = prepare(head)
        scores[at] = score(prepared[head], block)

    issue(0)
    pending = None
    for at, (head, block) in enumerate(tasks):
        if at + 1 < len(tasks):
            issue(at + 1)
        probs = softmax(scores.pop(at))
        if pending is not None:
            finish(*pending)
        pending = (prepared[head], block, probs)
    finish(*pending)
    if with_sums:
        sums = square_sums(y_ref[...])
        for copy in range(rest[0].shape[0]):
            rest[0][copy] = sums


def mixer(x, seq, total=None, row=0, gains=None, copies=0):
    width = x.shape[1]
    out_shape = [jax.ShapeDtypeStruct((seq, width), jnp.bfloat16)]
    if copies:
        out_shape.append(jax.ShapeDtypeStruct((copies, 1, seq), jnp.float32))
    plain = total is not None
    operands = (x, total, gains) if plain else (x,)
    whole = lambda array: pl.BlockSpec(array.shape, lambda i: (0,) * len(array.shape))
    out = pl.pallas_call(
        functools.partial(mixer_kernel, (plain, row, copies > 0)),
        grid=(1,),
        in_specs=[whole(operand) for operand in operands],
        out_specs=[whole(shape) for shape in out_shape],
        out_shape=out_shape,
        compiler_params=pltpu.CompilerParams(vmem_limit_bytes=VMEM_LIMIT),
        cost_estimate=FREE,
    )(*operands)
    return out if copies else out[0]


def place_kernel(*refs):
    out_ref = refs[-1]
    seq = out_ref.shape[1]
    slot, col = 0, 0
    for ref in refs[:-1]:
        out_ref[slot, :, col : col + ref.shape[1]] = ref[:seq]
        col += ref.shape[1]
        if col == out_ref.shape[2]:
            slot, col = slot + 1, 0


def place(parts, shape):
    return pl.pallas_call(
        place_kernel,
        in_specs=[pl.BlockSpec(memory_space=pltpu.VMEM)] * len(parts),
        out_specs=pl.BlockSpec(memory_space=pltpu.VMEM),
        out_shape=jax.ShapeDtypeStruct(shape, jnp.bfloat16),
        compiler_params=pltpu.CompilerParams(vmem_limit_bytes=VMEM_LIMIT),
        cost_estimate=FREE,
    )(*parts)


def moved(array, target):
    size = lax.axis_size("section")
    return lax.ppermute(array, "section", [(i, target(i) % size) for i in range(size)])


def summed(copies):
    return lax.psum(lax.all_to_all(copies, "z", 0, 0, tiled=True).sum(0), "xh")


def local(acts, plan, norm_gain, query_gain, key_gain, value_gain):
    half = lax.axis_size("section") // 2
    along = lax.axis_size("z")
    x = acts[0]
    seq, width = x.shape
    gains = (norm_gain[0], query_gain[0], key_gain[0], value_gain[0])
    behind = moved(x, lambda s: s + 2)
    now, later, copies, *parts = first(plan, gains, x, along)
    gains_later = moved(later, lambda s: s + 1)
    total, gains_later = lax.optimization_barrier((summed(copies), gains_later))
    packet, *far = packed(total, now, parts)
    packet = moved(packet, lambda s: s + 2)
    *far, behind, packet = lax.optimization_barrier((*far, behind, packet))
    mirror = [moved(part, lambda s: s + half) for part in far]

    once, copies = mixer(behind, seq, packet, 4, packet, copies=along)
    total = summed(copies)
    before, relayed = total, []
    for part in mirror:
        part, _ = lax.optimization_barrier((part, before))
        before = mixer(part, seq)
        relayed.append(moved(before, lambda s: s + 1))
    total, _ = lax.optimization_barrier((total, before))
    twice = mixer(once, seq, total, 0, gains_later)
    stash = place(mirror + relayed[:-1], (2, seq, width))
    stash = lax.dynamic_update_slice(stash, relayed[-1][None], (1, 0, width - FAR[-1]))
    return (twice[None], stash[None])


def solution(mesh):
    sections, shards = mesh.shape["section"], mesh.shape["tp"]
    fine = Mesh(mesh.devices.reshape(sections, 2, shards // 2), ("section", "xh", "z"))
    tp = ("xh", "z")
    gain = P("section", None, tp)
    return jax.shard_map(
        local,
        mesh=fine,
        in_specs=(P("section", None, tp), P(), gain, gain, gain, gain),
        out_specs=(P("section", None, tp), P("section", None, None, tp)),
        check_vma=False,
    )
```

```python
import functools
import math

import jax
import jax.numpy as jnp
from jax import lax
from jax.experimental import pallas as pl
from jax.experimental.pallas import tpu as pltpu
from jax.sharding import Mesh
from jax.sharding import PartitionSpec as P

D = 12288
HEAD = 128
BLOCK = 256
EPS = 1e-05
FAR = (256, 256, 256)
TAIL = 32
ACROSS_LAST = (((1,), (1,)), ((), ()))
VMEM_LIMIT = 52 * 2**20
FREE = pl.CostEstimate(flops=0, bytes_accessed=0, transcendentals=0)


def square_sums(y):
    yf = y.astype(jnp.float32)
    squared = yf * yf
    high = squared.astype(jnp.bfloat16)
    low = (squared - high.astype(jnp.float32)).astype(jnp.bfloat16)
    ones = jnp.ones((8, y.shape[1]), jnp.bfloat16)
    sums = lax.dot_general(ones, high, ACROSS_LAST, preferred_element_type=jnp.float32) + lax.dot_general(
        ones, low, ACROSS_LAST, preferred_element_type=jnp.float32
    )
    return sums[0:1]


def thirds(value):
    high = value.astype(jnp.bfloat16).astype(jnp.float32)
    middle = (value - high).astype(jnp.bfloat16).astype(jnp.float32)
    return [high, middle, value - high - middle]


def chosen(plan_ref, step, gains):
    lap = plan_ref[step, lax.axis_index("section")]
    return jnp.concatenate([jnp.where(lap == 0, gain[0:1], gain[1:2]) for gain in gains], axis=0)


def first_kernel(plan_ref, norm_ref, query_ref, key_ref, value_ref, x_ref, now_ref, later_ref, sums_ref, *part_refs):
    seq = x_ref.shape[0]
    gains = (norm_ref, query_ref, key_ref, value_ref)
    now = chosen(plan_ref, 0, gains)
    now_ref[...] = now
    sums = square_sums(x_ref[...])
    for copy in range(sums_ref.shape[0]):
        sums_ref[copy] = sums
    later_ref[...] = chosen(plan_ref, 1, gains)
    col = 0
    for part_ref in part_refs:
        part = part_ref.shape[1]
        cols = slice(col, col + part)
        part_ref[:seq] = x_ref[:, cols]
        tail = thirds(now[:, cols]) + [jnp.zeros((TAIL - 12, part), jnp.float32)]
        part_ref[seq:] = jnp.concatenate(tail, axis=0).astype(jnp.bfloat16)
        col += part


def first(plan, gains, x, copies):
    seq, width = x.shape
    gain = jax.ShapeDtypeStruct((4, width), jnp.float32)
    parts = tuple(jax.ShapeDtypeStruct((seq + TAIL, part), jnp.bfloat16) for part in FAR)
    return pl.pallas_call(
        first_kernel,
        in_specs=[pl.BlockSpec(memory_space=pltpu.SMEM)] + [pl.BlockSpec(memory_space=pltpu.VMEM)] * 5,
        out_shape=(gain, gain, jax.ShapeDtypeStruct((copies, 1, seq), jnp.float32)) + parts,
        compiler_params=pltpu.CompilerParams(vmem_limit_bytes=60 * 2**20),
        cost_estimate=FREE,
    )(plan, *gains, x)


def rows_of(value, width):
    count = -(-value.shape[1] // width)
    rest = count * width - value.shape[1]
    if rest:
        value = jnp.concatenate([value, jnp.zeros((1, rest), value.dtype)], axis=1)
    return [value[:, at * width : (at + 1) * width] for at in range(count)]


def pack_kernel(total_ref, now_ref, *refs):
    count = len(refs) // 2
    packet_ref = refs[count]
    packet_ref[0:4] = now_ref[...]
    packet_ref[4:5] = total_ref[...]
    for tail_ref, out_ref in zip(refs[:count], refs[count + 1 :]):
        part = out_ref.shape[1]
        rows = [piece for third in thirds(total_ref[...]) for piece in rows_of(third, part)]
        used = 12 + len(rows)
        tail = [tail_ref[0:12].astype(jnp.float32)] + rows + [jnp.zeros((TAIL - used, part), jnp.float32)]
        out_ref[...] = jnp.concatenate(tail, axis=0).astype(jnp.bfloat16)


def packed(total, now, parts):
    specs = [pl.BlockSpec((TAIL, part.shape[1]), lambda i, at=part.shape[0] // TAIL - 1: (at, 0)) for part in parts]
    whole = lambda shape: pl.BlockSpec(shape, lambda i: (0, 0))
    packet = (5, now.shape[1])
    return pl.pallas_call(
        pack_kernel,
        grid=(1,),
        in_specs=[whole(total.shape), whole(now.shape)] + specs,
        out_specs=[whole(packet)] + specs,
        out_shape=[jax.ShapeDtypeStruct(packet, jnp.float32)]
        + [jax.ShapeDtypeStruct(part.shape, part.dtype) for part in parts],
        input_output_aliases={2 + at: 1 + at for at in range(len(parts))},
        compiler_params=pltpu.CompilerParams(vmem_limit_bytes=60 * 2**20),
        cost_estimate=FREE,
    )(total, now, *parts)


def unpacked(part_ref, seq):
    tail = part_ref[seq:].astype(jnp.float32)
    gains = tail[0:4] + tail[4:8] + tail[8:12]
    count = -(-seq // part_ref.shape[1])
    rows = tail[12 : 12 + count] + tail[12 + count : 12 + 2 * count] + tail[12 + 2 * count : 12 + 3 * count]
    return gains, jnp.concatenate([rows[at : at + 1] for at in range(count)], axis=1)[:, :seq]


def mixer_kernel(config, x_ref, *refs):
    plain, row, with_sums = config
    if plain:
        total_ref, gain_ref, y_ref, rest = refs[0], refs[1], refs[2], refs[3:]
        total, gain = total_ref[row : row + 1], gain_ref[...]
    else:
        y_ref, rest = refs[0], refs[1:]
        gain, total = unpacked(x_ref, y_ref.shape[0])
    seq, width = y_ref.shape
    scale = lax.rsqrt(total / D + EPS)
    scale = jnp.transpose(jnp.broadcast_to(scale, (8, seq)))[:, 0:1]
    factor = math.log2(math.e) / math.sqrt(HEAD)
    causal = lax.broadcasted_iota(jnp.int32, (BLOCK, BLOCK), 1) <= lax.broadcasted_iota(
        jnp.int32, (BLOCK, BLOCK), 0
    )

    def prepare(head):
        cols = slice(head * HEAD, (head + 1) * HEAD)
        normed = x_ref[:seq, cols].astype(jnp.float32) * scale * gain[0:1, cols]
        query = (normed * gain[1:2, cols]).astype(jnp.bfloat16)
        keys = (normed * gain[2:3, cols]).astype(jnp.bfloat16)
        return query, keys, normed.astype(jnp.bfloat16), gain[3:4, cols], cols

    def score(ready, block):
        query, keys = ready[:2]
        lo, hi = block * BLOCK, (block + 1) * BLOCK
        raw = lax.dot_general(query[lo:hi], keys[:hi], ACROSS_LAST, preferred_element_type=jnp.float32)
        last = jnp.where(causal, raw[:, lo:], -1e30)
        return jnp.concatenate([raw[:, :lo], last], axis=1) if lo else last

    def softmax(raw):
        top = jnp.max(raw, axis=1, keepdims=True)
        weights = jnp.exp2((raw - top) * factor)
        return (weights * (1.0 / jnp.sum(weights, axis=1, keepdims=True))).astype(jnp.bfloat16)

    def finish(ready, block, probs):
        values, value_gain, cols = ready[2:]
        lo, hi = block * BLOCK, (block + 1) * BLOCK
        att = jnp.dot(probs, values[:hi], preferred_element_type=jnp.float32)
        y_ref[lo:hi, cols] = (
            x_ref[lo:hi, cols].astype(jnp.float32) + value_gain * att
        ).astype(jnp.bfloat16)

    tasks = [(head, block) for head in range(width // HEAD) for block in range(seq // BLOCK)]
    prepared = {}
    scores = {}

    def issue(at):
        head, block = tasks[at]
        if head not in prepared:
            prepared[head] = prepare(head)
        scores[at] = score(prepared[head], block)

    issue(0)
    pending = None
    for at, (head, block) in enumerate(tasks):
        if at + 1 < len(tasks):
            issue(at + 1)
        probs = softmax(scores.pop(at))
        if pending is not None:
            finish(*pending)
        pending = (prepared[head], block, probs)
    finish(*pending)
    if with_sums:
        sums = square_sums(y_ref[...])
        for copy in range(rest[0].shape[0]):
            rest[0][copy] = sums


def mixer(x, seq, total=None, row=0, gains=None, copies=0):
    width = x.shape[1]
    out_shape = [jax.ShapeDtypeStruct((seq, width), jnp.bfloat16)]
    if copies:
        out_shape.append(jax.ShapeDtypeStruct((copies, 1, seq), jnp.float32))
    plain = total is not None
    operands = (x, total, gains) if plain else (x,)
    whole = lambda array: pl.BlockSpec(array.shape, lambda i: (0,) * len(array.shape))
    out = pl.pallas_call(
        functools.partial(mixer_kernel, (plain, row, copies > 0)),
        grid=(1,),
        in_specs=[whole(operand) for operand in operands],
        out_specs=[whole(shape) for shape in out_shape],
        out_shape=out_shape,
        compiler_params=pltpu.CompilerParams(vmem_limit_bytes=VMEM_LIMIT),
        cost_estimate=FREE,
    )(*operands)
    return out if copies else out[0]


def place_kernel(*refs):
    out_ref = refs[-1]
    seq = out_ref.shape[1]
    slot, col = 0, 0
    for ref in refs[:-1]:
        out_ref[slot, :, col : col + ref.shape[1]] = ref[:seq]
        col += ref.shape[1]
        if col == out_ref.shape[2]:
            slot, col = slot + 1, 0


def place(parts, shape):
    return pl.pallas_call(
        place_kernel,
        in_specs=[pl.BlockSpec(memory_space=pltpu.VMEM)] * len(parts),
        out_specs=pl.BlockSpec(memory_space=pltpu.VMEM),
        out_shape=jax.ShapeDtypeStruct(shape, jnp.bfloat16),
        compiler_params=pltpu.CompilerParams(vmem_limit_bytes=VMEM_LIMIT),
        cost_estimate=FREE,
    )(*parts)


def moved(array, target):
    size = lax.axis_size("section")
    return lax.ppermute(array, "section", [(i, target(i) % size) for i in range(size)])


def summed(copies):
    return lax.psum(lax.all_to_all(copies, "z", 0, 0, tiled=True).sum(0), "xh")


def local(acts, plan, norm_gain, query_gain, key_gain, value_gain):
    half = lax.axis_size("section") // 2
    along = lax.axis_size("z")
    x = acts[0]
    seq, width = x.shape
    gains = (norm_gain[0], query_gain[0], key_gain[0], value_gain[0])
    behind = moved(x, lambda s: s + 2)
    now, later, copies, *parts = first(plan, gains, x, along)
    gains_later = moved(later, lambda s: s + 1)
    total, gains_later = lax.optimization_barrier((summed(copies), gains_later))
    packet, *far = packed(total, now, parts)
    packet = moved(packet, lambda s: s + 2)
    *far, behind, packet = lax.optimization_barrier((*far, behind, packet))
    mirror = [moved(part, lambda s: s + half) for part in far]

    once, copies = mixer(behind, seq, packet, 4, packet, copies=along)
    total = summed(copies)
    before, relayed = total, []
    for part in mirror:
        part, _ = lax.optimization_barrier((part, before))
        before = mixer(part, seq)
        relayed.append(moved(before, lambda s: s + 1))
    total, _ = lax.optimization_barrier((total, before))
    twice = mixer(once, seq, total, 0, gains_later)
    stash = place(mirror + relayed[:-1], (2, seq, width))
    stash = lax.dynamic_update_slice(stash, relayed[-1][None], (1, 0, width - FAR[-1]))
    return (twice[None], stash[None])


def solution(mesh):
    sections, shards = mesh.shape["section"], mesh.shape["tp"]
    fine = Mesh(mesh.devices.reshape(sections, 2, shards // 2), ("section", "xh", "z"))
    tp = ("xh", "z")
    gain = P("section", None, tp)
    return jax.shard_map(
        local,
        mesh=fine,
        in_specs=(P("section", None, tp), P(), gain, gain, gain, gain),
        out_specs=(P("section", None, tp), P("section", None, None, tp)),
        check_vma=False,
    )
```
